256 devices in a mesh: grp: 16 (over x, y), dev: 16 (over z, core).
Axes of the slice: x: 4, y: 4, z: 8, core: 2. Of those that a mesh axis runs over, the one named last changes fastest.
Arguments:
- rows: bfloat16 [2, 32768, 384], P(None, ('grp', 'dev')), may hold values from -6 to 6
- adj_rhs: float32 [2, 32768, 256], P(None, ('grp', 'dev')), may hold values from -6 to 6
- pattern: int32 [32768, 24], P(('grp', 'dev')), may hold values from 0 to 2559
- lengths: int32 [32768], P(('grp', 'dev')), may hold values from 6 to 24, as said below
Outputs:
- applied: float32 [2, 32768, 256], P(None, ('grp', 'dev'))
The draws below stay inside these ranges and needn't reach their ends.
Inputs may be any that keep to these rules, and one draw needn't show every extreme that they name: `lengths`: every device's first block row uses all 24 entries.
All inputs are finite; a program needn't handle non-finite values.
Results may differ from the reference program's by a relative error of at most 0.0006.
Values may be sent and summed in bfloat16 or wider, within the bound.
A program may use at most 128 MiB of HBM per device.

```python
import jax
import jax.numpy as jnp
from jax import lax

WIDTH = 384
SLOTS = 24
OBJECTIVES = 256
POINTS = 2
ROW_DEV = 128
GHOST = 16
ROWS = 32768
N_GRP = 16
N_DEV = 16


def draw_lengths(key, part):
    key = jax.random.fold_in(key, 1)
    values = jax.random.randint(key, (ROWS,), SLOTS // 4, SLOTS + 1).astype(jnp.int32)
    return values.at[::ROW_DEV].set(SLOTS)


def place_ends(result, key, least, high):
    place = [jax.random.randint(jax.random.fold_in(key, axis), (), 0, length) for axis, length in enumerate(result.shape)]
    widest = result.shape.index(max(result.shape))
    beside = place[:widest] + [(place[widest] + 1) % result.shape[widest]] + place[widest + 1:]
    return result.at[tuple(place)].set(least).at[tuple(beside)].set(high)


def levels(own_key, dims, pieces, smallest, top_value):
    gain, own = 1.0, jax.random.fold_in(own_key, 6)
    for axis_at, parts in pieces:
        draws = jnp.exp(jax.random.uniform(jax.random.fold_in(own, axis_at), (parts,), jnp.float32, smallest / len(pieces), top_value / len(pieces)))
        gain = gain * jnp.repeat(draws, dims[axis_at] // parts).reshape([-1 if axis == axis_at else 1 for axis in range(len(dims))])
    return gain


def gaussian(rng, dims, scale, most, split=(), kind=jnp.bfloat16):
    result = scale * jax.random.normal(rng, dims, jnp.float32)
    if split:
        result = result * levels(rng, dims, split, -0.22, 0.18)
    return jnp.clip(result, -most, most).astype(kind)


def setup_inputs(seed: int = 0) -> dict:
    keys = jax.random.split(jax.random.key(seed), 5)
    rows = gaussian(keys[0], (POINTS, ROWS, WIDTH), 1.0, 6.0, ((1, 256),))
    adj_rhs = gaussian(keys[1], (POINTS, ROWS, OBJECTIVES), 1.0, 6.0, ((1, 256),), jnp.float32)
    pattern = place_ends(jax.random.randint(keys[2], (ROWS, SLOTS), 0, N_DEV * (ROW_DEV + 2 * GHOST)), jax.random.fold_in(keys[2], 1), 0, (N_DEV * (ROW_DEV + 2 * GHOST)) - 1).astype(jnp.int32)
    lengths = draw_lengths(jax.random.fold_in(keys[4], 71), 0)
    return dict(rows=rows, adj_rhs=adj_rhs, pattern=pattern, lengths=lengths)


ridge_share = 0.25

def reference(rows, adj_rhs, pattern, lengths):
    ext_rows = ROW_DEV + 2 * GHOST
    glob = jnp.arange(ROWS, dtype=jnp.int32)
    group = (glob // (N_DEV * ROW_DEV))[:, None]
    owner = pattern // ext_rows
    inside = pattern % ext_rows
    src_group = jnp.where(inside < ROW_DEV, group, jnp.where(inside < ROW_DEV + GHOST, (group - 1) % N_GRP, (group + 1) % N_GRP))
    src_local = jnp.where(inside < ROW_DEV, inside, jnp.where(inside < ROW_DEV + GHOST, inside - ROW_DEV, inside - ROW_DEV - GHOST))
    source = ((src_group * N_DEV + owner) * ROW_DEV + src_local).astype(jnp.int32)
    used = jnp.arange(SLOTS, dtype=jnp.int32)[None, :] < lengths[:, None]
    eye = jnp.eye(SLOTS, dtype=jnp.float32)

    def one_block(block):
        first = (block * ROW_DEV).astype(jnp.int32)
        idx = lax.dynamic_slice_in_dim(source, first, ROW_DEV, 0)
        msk = lax.dynamic_slice_in_dim(used, first, ROW_DEV, 0)
        own = lax.dynamic_slice_in_dim(rows, first, ROW_DEV, 1).astype(jnp.float32)
        near = jnp.take(rows, idx, axis=1).astype(jnp.float32)
        near = jnp.where(msk[None, :, :, None], near, 0.0)
        gram = jnp.einsum('prkw,prjw->prkj', near, near, precision=lax.Precision.HIGHEST)
        gram = gram + ridge_share * WIDTH * eye
        target = jnp.einsum('prkw,prw->prk', near, own, precision=lax.Precision.HIGHEST)
        factor = jnp.linalg.cholesky(gram)
        return jax.scipy.linalg.cho_solve((factor, True), target[..., None])[..., 0]
    coeff = lax.map(one_block, jnp.arange(ROWS // ROW_DEV, dtype=jnp.int32))
    coeff = jnp.transpose(coeff, (1, 0, 2, 3)).reshape(POINTS, ROWS, SLOTS)

    def add_slot(slot, total):
        column = lax.dynamic_index_in_dim(source, slot, 1, keepdims=False)
        weight = lax.dynamic_index_in_dim(coeff, slot, 2, keepdims=False)
        return total.at[:, column].add(weight[:, :, None] * adj_rhs)
    summed = lax.fori_loop(0, SLOTS, add_slot, jnp.zeros_like(adj_rhs))
    return adj_rhs - summed
```

```python
import functools

import jax
import jax.numpy as jnp
from jax import lax
from jax.experimental import pallas as pl
from jax.experimental.pallas import tpu as pltpu
from jax.sharding import PartitionSpec as P

GHOST = 16
ridge_share = 0.25

MESH = pl.DeviceIdType.MESH
F32 = jnp.float32
BF16 = jnp.bfloat16
MEMBERS = 5
LANES = 128
PER_STEP = 832


class Copies:
    def __init__(self, send, recv):
        self.send, self.recv, self.started = send, recv, []

    def start(self, src, dst, device):
        at = len(self.started)
        copy = pltpu.make_async_remote_copy(
            src_ref=src, dst_ref=dst, send_sem=self.send.at[at], recv_sem=self.recv.at[at],
            device_id=device, device_id_type=MESH,
        )
        copy.start()
        self.started.append(copy)
        return at

    def arrived(self, at, dst, device):
        pltpu.make_async_remote_copy(
            src_ref=dst, dst_ref=dst, send_sem=self.send.at[at], recv_sem=self.recv.at[at],
            device_id=device, device_id_type=MESH,
        ).wait_recv()

    def finish(self):
        for copy in self.started:
            copy.wait_send()


def kernel(dims, rows_ref, adj_ref, pat_ref, out_ref, pool, ghost, idxb, near, adjg, adj_low, coefg, gram, mat,
           tbuf, acc, back, send_sems, recv_sems):
    n_grp, n_dev, points, own, width, slots, objs = dims
    n_z = n_dev // 2
    far = n_z // 2
    ext = own + 2 * GHOST
    n_groups = near.shape[0] // LANES
    me_g, me_d = lax.axis_index("grp"), lax.axis_index("dev")
    z, c = lax.div(me_d, 2), lax.rem(me_d, 2)
    other = 1 - c

    def chip(step):
        return lax.rem(z + step + n_z, n_z)

    right = {"dev": chip(1) * 2 + c}
    left = {"dev": chip(-1) * 2 + c}
    partner = {"dev": z * 2 + other}
    above = {"grp": lax.rem(me_g + 1, n_grp)}
    below = {"grp": lax.rem(me_g + n_grp - 1, n_grp)}
    ring = (right, left)
    copies = Copies(send_sems, recv_sems)

    barrier = pltpu.get_barrier_semaphore()
    for device in (right, left, partner, above, below):
        pl.semaphore_signal(barrier, inc=1, device_id=device, device_id_type=MESH)

    def block(zz, cc, at=0, size=None):
        size = own if size is None else size
        return pool.at[zz, pl.ds(pl.multiple_of(cc * own + at, 16), size), :]

    for p in range(points):
        pool[z, pl.ds(pl.multiple_of(c * own, own), own), p * width : (p + 1) * width] = rows_ref[p]
    pl.semaphore_wait(barrier, 5)

    half = own // 2
    waiting_ghost = []

    def pass_ghost(zz, cc):
        at = pl.ds(pl.multiple_of((zz * 2 + cc) * GHOST, GHOST), GHOST)
        src = block(zz, cc, 0, GHOST)
        waiting_ghost.append((copies.start(src, ghost.at[0, at, :], above), 0, at, above))
        waiting_ghost.append((copies.start(src, ghost.at[1, at, :], below), 1, at, below))

    def forward_row(flow, zz, part):
        ref = block(zz, c, part * half, half)
        return copies.start(ref, ref, ring[flow])

    def share_row(zz):
        ref = block(zz, c)
        return copies.start(ref, ref, partner)

    pieces = {}
    for part in (0, 1):
        for flow in (0, 1):
            if far > 1 or part == flow:
                pieces[flow, part] = forward_row(flow, z, part)
    shared = [(share_row(z), z)]
    pass_ghost(z, c)

    pat = pat_ref[...]
    owner = jnp.floor((pat + 0.5) * (1.0 / ext))
    inside = pat - owner * ext
    place = jnp.where(
        inside < own,
        owner * own + inside,
        jnp.where(inside < own + GHOST, owner * GHOST + inside + (n_dev * own - own),
                  owner * GHOST + inside + (n_dev * (own + GHOST) - own - GHOST)),
    )
    place = jnp.where(pat < 0, -1.0, place)
    first_own = (me_d * own).astype(F32)
    sub8 = lax.broadcasted_iota(jnp.int32, (8, LANES), 0).astype(F32)

    def fill_index(m, carry):
        rolled = pltpu.roll(place, lax.rem(LANES - m, LANES), 1)
        base = pl.multiple_of(m * LANES, LANES)
        for member in range(MEMBERS):
            first = member * n_groups
            column = jnp.broadcast_to(rolled[:, first : first + 1], (slots, LANES))
            if first + n_groups > own:
                column = jnp.where(first + m < own, column, -1.0)
            idxb[pl.ds(base + member * slots, slots), :] = column
        mine = sub8 * n_groups + m.astype(F32)
        mine = jnp.where((sub8 < MEMBERS) & (mine < own), mine + first_own, -1.0)
        idxb[pl.ds(base + MEMBERS * slots, 8), :] = mine
        return carry

    lax.fori_loop(0, n_groups, fill_index, 0)

    code_rows = 16
    adj_rows = own + code_rows

    def adj_block(zz, at=0, size=None):
        size = adj_rows if size is None else size
        return adjg.at[zz, pl.ds(pl.multiple_of(c * adj_rows + at, 16), size), :]

    adj_at = pl.ds(pl.multiple_of(code_rows + c * own, 16), own)
    for p in range(points):
        cut = slice(p * objs, (p + 1) * objs)
        high = adj_ref[p].astype(BF16)
        adjg[z, adj_at, cut] = high
        adj_low[:, cut] = (adj_ref[p] - high.astype(F32)).astype(BF16)
    code_at = pl.ds(pl.multiple_of(c * (2 * own + code_rows), 16), code_rows)
    for j in range(slots // 8):
        cut = slice(8 * j, 8 * j + 8)
        codes = jnp.concatenate([owner[cut], inside[cut]], axis=0)
        adjg[z, code_at, j * LANES : (j + 1) * LANES] = codes.astype(BF16)

    def add_tiles(tiles, first=False):
        def body(step, carry):
            at = pl.ds(pl.multiple_of(step * PER_STEP, PER_STEP), PER_STEP)
            index = idxb[at, :]
            total = None
            for load, base, depth in tiles:
                base = jnp.asarray(base, jnp.int32).astype(F32)
                relative = index - base
                parts = []
                for lane in range(0, depth, LANES):
                    wide = min(LANES, depth - lane)
                    lanes = (lax.broadcasted_iota(jnp.int32, (PER_STEP, wide), 1) + lane).astype(F32)
                    parts.append(jnp.where(relative[:, :wide] == lanes, 1.0, 0.0).astype(BF16))
                hot = parts[0] if len(parts) == 1 else jnp.concatenate(parts, axis=1)
                product = jnp.dot(hot, load(), preferred_element_type=F32)
                total = product if total is None else total + product
            total = total.astype(BF16)
            near[at, :] = total if first else near[at, :] + total
            return carry

        lax.fori_loop(0, near.shape[0] // PER_STEP, body, 0)

    def chip_tile(zz):
        return (lambda: pool[zz]), zz * (2 * own), 2 * own

    def take_shared(found):
        for at, zz in found:
            copies.arrived(at, block(zz, other), partner)
            pass_ghost(zz, other)

    take_shared(shared)
    add_tiles([chip_tile(z)], first=True)
    for hop in range(1, far + 1):
        last = hop == far
        from_left, from_right = chip(-hop), chip(hop)
        later = {}
        shared = []
        for part in (0, 1):
            for flow, zz in ((0, from_left), (1, from_right)):
                if (flow, part) not in pieces:
                    continue
                copies.arrived(pieces[flow, part], block(zz, c, part * half, half), ring[flow])
                if hop < far - 1 or (hop == far - 1 and part == flow):
                    later[flow, part] = forward_row(flow, zz, part)
                if not last and part == 0:
                    pass_ghost(zz, c)
        if last:
            shared.append((share_row(from_left), from_left))
            pass_ghost(from_left, c)
        else:
            shared.append((share_row(from_left), from_left))
            shared.append((share_row(from_right), from_right))
        pieces = later
        if last:
            break
        take_shared(shared)
        add_tiles([chip_tile(from_left), chip_tile(from_right)])

    adj_first = adj_rows // 2 // 16 * 16
    adj_cut = ((0, adj_first), (adj_first, adj_rows - adj_first))
    adj_state = {"sent": {}, "shared": []}

    def adj_send(zz, hop):
        for flow, block_of in zz:
            if hop == far:
                ref = adj_block(block_of, *adj_cut[flow])
            else:
                ref = adj_block(block_of)
            adj_state["sent"][flow, hop] = copies.start(ref, ref, ring[flow])

    def adj_share(zz):
        ref = adj_block(zz)
        adj_state["shared"].append((copies.start(ref, ref, partner), zz))

    def adj_step(hop):
        both = ((0, chip(-hop)), (1, chip(hop)))
        for flow, zz in both:
            ref = adj_block(zz, *adj_cut[flow]) if hop == far else adj_block(zz)
            copies.arrived(adj_state["sent"][flow, hop], ref, ring[flow])
            if hop < far:
                adj_send([(flow, zz)], hop + 1)
                adj_share(zz)
        if hop == far:
            adj_share(chip(hop))

    adj_send([(0, z), (1, z)], 1)
    adj_share(z)
    take_shared(shared)
    add_tiles([chip_tile(chip(far))])
    adj_step(1)
    for at, side, where, device in waiting_ghost:
        copies.arrived(at, ghost.at[side, where, :], device)
    side_rows = n_dev * GHOST
    add_tiles([
        ((lambda: ghost[0]), n_dev * own, side_rows),
        ((lambda: ghost[1]), n_dev * own + side_rows, side_rows),
    ])
    if far >= 2:
        adj_step(2)

    lane = lax.broadcasted_iota(jnp.int32, (slots, LANES), 1)
    sub = lax.broadcasted_iota(jnp.int32, (slots, LANES), 0)
    ridge = jnp.zeros((slots, LANES), F32)
    for member in range(MEMBERS):
        ridge = jnp.where(lane - member * slots == sub, ridge_share * width, ridge)
    lane8 = lax.broadcasted_iota(jnp.int32, (8, LANES), 1)
    row8 = lax.broadcasted_iota(jnp.int32, (8, LANES), 0)
    own_mask = (lane8 >= row8 * slots) & (lane8 < row8 * slots + slots)

    def make_gram(m, carry):
        tile = near[pl.ds(pl.multiple_of(m * LANES, LANES), LANES), :]
        for p in range(points):
            part = tile[:, p * width : (p + 1) * width]
            full = lax.dot_general(part, part, (((1,), (1,)), ((), ())), preferred_element_type=F32)
            packed = full[:slots]
            for member in range(1, MEMBERS):
                packed = jnp.where(lane >= member * slots, full[member * slots : (member + 1) * slots], packed)
            at = (p * 32 + m) * 32
            gram[pl.ds(pl.multiple_of(at, 32), slots), :] = packed + ridge
            target = jnp.sum(jnp.where(own_mask, full[MEMBERS * slots :], 0.0), axis=0, keepdims=True)
            gram[pl.ds(pl.multiple_of(at + slots, 8), 8), :] = jnp.broadcast_to(target, (8, LANES))
        return carry

    lax.fori_loop(0, n_groups, make_gram, 0)
    if far >= 3:
        adj_step(3)

    for i in range(slots + 1):
        turned = jnp.transpose(gram[pl.ds(i, 64, stride=32), :])
        mat[i, :, :, 0:64] = turned[: MEMBERS * slots].reshape(MEMBERS, slots, 64)

    for j0 in range(0, slots, 8):
        span = slots - j0
        at_slot = lax.broadcasted_iota(jnp.int32, (MEMBERS, span, LANES), 1) + j0

        def eliminate(step, carry):
            col = step + j0
            pivot_row = mat[col, :, j0:slots, :]
            inverse = 1.0 / mat[col, :, pl.ds(col, 1), :]
            beyond = at_slot > col
            factors = jnp.where(beyond, pivot_row * inverse, 0.0)
            for i in range(j0, slots):
                block_at = i // 8 * 8
                mat[i, :, block_at:slots, :] = (
                    mat[i, :, block_at:slots, :] - factors[:, i - j0 : i - j0 + 1, :] * pivot_row[:, block_at - j0 :, :]
                )
            rhs = mat[slots, :, pl.ds(col, 1), :]
            mat[slots, :, j0:slots, :] = mat[slots, :, j0:slots, :] - rhs * factors
            return carry

        lax.fori_loop(0, 8, eliminate, 0)

    at_slot = lax.broadcasted_iota(jnp.int32, (MEMBERS, slots, LANES), 1)
    solved = jnp.zeros((MEMBERS, slots, LANES), F32)
    for col in range(slots - 1, -1, -1):
        line = mat[col]
        inverse = 1.0 / line[:, col : col + 1, :]
        scaled = jnp.where(at_slot > col, line * inverse, 0.0)
        known = jnp.sum(scaled * solved, axis=1, keepdims=True)
        value = mat[slots, :, col : col + 1, :] * inverse - known
        solved = jnp.where(at_slot == col, value, solved)

    coef_rows = points * slots

    def coef_block(zz, cc, at=0, size=None):
        size = coef_rows if size is None else size
        return coefg.at[zz, pl.ds(pl.multiple_of(cc * coef_rows + at, 8), size), :]

    for p in range(points):
        coeff = jnp.zeros((slots, LANES), F32)
        for member in range(MEMBERS):
            first = member * n_groups
            rolled = pltpu.roll(solved[member], (first - 32 * p) % LANES, 1)
            coeff = jnp.where((lane >= first) & (lane < first + n_groups), rolled, coeff)
        coefg[z, pl.ds(pl.multiple_of(c * coef_rows + p * slots, 8), slots), :] = coeff

    def coef_send(flow, zz, hop):
        ref = coef_block(zz, c, flow * slots, slots) if hop == far else coef_block(zz, c)
        return copies.start(ref, ref, ring[flow])

    def coef_share(zz):
        ref = coef_block(zz, c)
        return copies.start(ref, ref, partner)

    sent = {flow: coef_send(flow, z, 1) for flow in (0, 1)}
    shared = [(coef_share(z), z)]
    for hop in range(4, far + 1):
        adj_step(hop)
    for at, zz in adj_state["shared"]:
        copies.arrived(at, adjg.at[zz, pl.ds(pl.multiple_of(other * adj_rows, 16), adj_rows), :], partner)

    me_f = me_d.astype(F32)
    entry = lax.broadcasted_iota(jnp.int32, (ext, LANES), 0).astype(F32)

    def make_table(slot_of, zz, cc):
        code_at = pl.multiple_of(cc * (2 * own + code_rows), 16)
        picked = []
        for j in range(slots // 8):
            codes = adjg[zz, pl.ds(code_at, code_rows), j * LANES : (j + 1) * LANES].astype(F32)
            picked.append(jnp.where(codes[:8] == me_f, codes[8:], -1.0))
        weights = coefg[zz, pl.ds(pl.multiple_of(cc * coef_rows, 8), coef_rows), :]
        tables = [jnp.zeros((ext, LANES), F32) for _ in range(points)]
        for k in range(slots):
            match = picked[k // 8][k % 8 : k % 8 + 1] == entry
            for p in range(points):
                row = p * slots + k
                tables[p] = tables[p] + jnp.where(match, weights[row : row + 1], 0.0)
        for p in range(points):
            tbuf[slot_of, p, :, pl.ds(pl.multiple_of(cc * LANES, LANES), LANES)] = tables[p]

    def multiply(slot_of, zz, first=False):
        for p in range(points):
            table = tbuf[slot_of, p]
            high = table.astype(BF16)
            low = (table - high.astype(F32)).astype(BF16)
            right_side = adjg[zz, code_rows : code_rows + 2 * own, p * objs : (p + 1) * objs]
            product = jnp.dot(high, right_side, preferred_element_type=F32)
            product += jnp.dot(low, right_side, preferred_element_type=F32)
            if first:
                mine = tbuf[slot_of, p, :, pl.ds(pl.multiple_of(c * LANES, LANES), LANES)].astype(BF16)
                product += jnp.dot(mine, adj_low[:, p * objs : (p + 1) * objs], preferred_element_type=F32)
            acc[p] = product if first else acc[p] + product

    make_table(0, z, c)
    at, zz = shared[0]
    copies.arrived(at, coef_block(zz, other), partner)
    make_table(0, z, other)
    multiply(0, z, first=True)
    for hop in range(1, far + 1):
        from_left, from_right = chip(-hop), chip(hop)
        shared, later = [], {}
        for flow, zz in ((0, from_left), (1, from_right)):
            ref = coef_block(zz, c, flow * slots, slots) if hop == far else coef_block(zz, c)
            copies.arrived(sent[flow], ref, ring[flow])
            if hop < far:
                later[flow] = coef_send(flow, zz, hop + 1)
                shared.append((coef_share(zz), zz))
        if hop == far:
            shared.append((coef_share(from_left), from_left))
        sent = later
        count = len(shared)

        def tile_of(i):
            return jnp.where(i == 0, from_left, from_right)

        def near_half(i, carry):
            make_table(i, tile_of(i), c)
            return carry

        def far_half(i, carry):
            make_table(i, tile_of(i), other)
            multiply(i, tile_of(i))
            return carry

        lax.fori_loop(0, count, near_half, 0)
        for at, zz in shared:
            copies.arrived(at, coef_block(zz, other), partner)
        lax.fori_loop(0, count, far_half, 0)

    low_rows, high_rows = acc.at[:, own : own + GHOST, :], acc.at[:, own + GHOST : ext, :]
    from_above = copies.start(low_rows, back.at[0], below)
    from_below = copies.start(high_rows, back.at[1], above)
    out_ref[...] = adj_ref[...] - acc[:, :own, :]
    copies.arrived(from_above, back.at[0], below)
    copies.arrived(from_below, back.at[1], above)
    out_ref[:, :GHOST, :] = out_ref[:, :GHOST, :] - (back[0] + back[1])
    copies.finish()


def local(rows, adj_rhs, pattern, lengths):
    points, own, width = rows.shape
    slots = pattern.shape[1]
    objs = adj_rhs.shape[2]
    n_grp, n_dev = lax.axis_size("grp"), lax.axis_size("dev")
    n_z = n_dev // 2
    n_groups = -(-own // MEMBERS)
    ext = own + 2 * GHOST
    used = jnp.arange(slots, dtype=jnp.int32)[:, None] < lengths[None, :]
    masked = jnp.where(used, pattern.T, -1).astype(F32)
    n_copies = 160
    vmem = pl.BlockSpec(memory_space=pltpu.VMEM)
    return pl.pallas_call(
        functools.partial(kernel, (n_grp, n_dev, points, own, width, slots, objs)),
        out_shape=jax.ShapeDtypeStruct(adj_rhs.shape, F32),
        in_specs=[vmem] * 3,
        out_specs=vmem,
        scratch_shapes=[
            pltpu.VMEM((n_z, 2 * own, points * width), BF16),
            pltpu.VMEM((2, n_dev * GHOST, points * width), BF16),
            pltpu.VMEM((n_groups * LANES, LANES), F32),
            pltpu.VMEM((n_groups * LANES, points * width), BF16),
            pltpu.VMEM((n_z, 2 * own + 32, points * objs), BF16),
            pltpu.VMEM((own, points * objs), BF16),
            pltpu.VMEM((n_z, 2 * points * slots, LANES), F32),
            pltpu.VMEM((64 * 32, LANES), F32),
            pltpu.VMEM((slots + 1, MEMBERS, slots, LANES), F32),
            pltpu.VMEM((2, points, ext, 2 * own), F32),
            pltpu.VMEM((points, ext, objs), F32),
            pltpu.VMEM((2, points, GHOST, objs), F32),
            pltpu.SemaphoreType.DMA((n_copies,)),
            pltpu.SemaphoreType.DMA((n_copies,)),
        ],
        compiler_params=pltpu.CompilerParams(
            collective_id=0, has_side_effects=True, vmem_limit_bytes=48 * 1024 * 1024
        ),
    )(rows, adj_rhs, masked)


def solution(mesh):
    placed = (
        P(None, ("grp", "dev"), None),
        P(None, ("grp", "dev"), None),
        P(("grp", "dev"), None),
        P(("grp", "dev")),
    )
    return jax.shard_map(
        local, mesh=mesh, in_specs=placed, out_specs=P(None, ("grp", "dev"), None), check_vma=False
    )
```

```python
import functools

import jax
import jax.numpy as jnp
from jax import lax
from jax.experimental import pallas as pl
from jax.experimental.pallas import tpu as pltpu
from jax.sharding import PartitionSpec as P

GHOST = 16
ridge_share = 0.25

MESH = pl.DeviceIdType.MESH
F32 = jnp.float32
BF16 = jnp.bfloat16
MEMBERS = 5
LANES = 128
PER_STEP = 3328
UNROLL_INDEX = 13
TURNS = 4
UNROLL_GRAM = 13


class Copies:
    def __init__(self, send, recv):
        self.send, self.recv, self.started, self.gone = send, recv, [], set()

    def start(self, src, dst, device):
        at = len(self.started)
        copy = pltpu.make_async_remote_copy(
            src_ref=src, dst_ref=dst, send_sem=self.send.at[at], recv_sem=self.recv.at[at],
            device_id=device, device_id_type=MESH,
        )
        copy.start()
        self.started.append(copy)
        return at

    def arrived(self, at, dst, device):
        pltpu.make_async_remote_copy(
            src_ref=dst, dst_ref=dst, send_sem=self.send.at[at], recv_sem=self.recv.at[at],
            device_id=device, device_id_type=MESH,
        ).wait_recv()

    def left(self, at):
        self.started[at].wait_send()
        self.gone.add(at)

    def finish(self):
        for at, copy in enumerate(self.started):
            if at not in self.gone:
                copy.wait_send()


def kernel(dims, rows_ref, adj_ref, pat_ref, len_ref, out_ref, pool, ghost, idxb, near, adjg, adj_low, coefg, gram, mat,
           tall, adj_own, acc, back, send_sems, recv_sems, load_sems):
    n_grp, n_dev, points, own, width, slots, objs = dims
    n_z = n_dev // 2
    far = n_z // 2
    ext = own + 2 * GHOST
    n_groups = near.shape[0] // LANES
    me_g, me_d = lax.axis_index("grp"), lax.axis_index("dev")
    z, c = lax.div(me_d, 2), lax.rem(me_d, 2)
    other = 1 - c

    def chip(step):
        return lax.rem(z + step + n_z, n_z)

    def peer(step):
        return {"dev": chip(step) * 2 + c}

    right, left = peer(1), peer(-1)
    partner = {"dev": z * 2 + other}
    above, below = lax.rem(me_g + 1, n_grp), lax.rem(me_g + n_grp - 1, n_grp)
    sides = (above, below)
    ring = (right, left)
    copies = Copies(send_sems, recv_sems)

    barrier = pltpu.get_barrier_semaphore()
    greeted = [peer(step) for step in range(1, n_z)] + [partner]
    for side in sides:
        greeted += [{"grp": side}, {"grp": side, "dev": z * 2 + other}, {"grp": side, "dev": chip(far) * 2 + c}]
    for device in greeted:
        pl.semaphore_signal(barrier, inc=1, device_id=device, device_id_type=MESH)

    def block(zz, cc, at=0, size=None):
        size = own if size is None else size
        return pool.at[zz, pl.ds(pl.multiple_of(cc * own + at, 16), size), :]

    mine_at = pl.ds(pl.multiple_of(c * own, own), own)
    loads = [
        pltpu.make_async_copy(rows_ref.at[p], pool.at[z, mine_at, pl.ds(p * width, width)], load_sems.at[p])
        for p in range(points)
    ]
    adj_load = pltpu.make_async_copy(adj_ref, adj_own, load_sems.at[points])
    for load in loads:
        load.start()
    adj_load.start()
    pat = pat_ref[...].astype(F32)
    pat = jnp.transpose(jnp.concatenate([pat, jnp.zeros((own, LANES - slots), F32)], axis=1))[:slots]
    slot_of = lax.broadcasted_iota(jnp.int32, (slots, own), 0)
    pat = jnp.where(slot_of < len_ref[...], pat, -1.0)
    owner = jnp.floor((pat + 0.5) * (1.0 / ext))
    inside = pat - owner * ext
    place = jnp.where(
        inside < own,
        owner * own + inside,
        jnp.where(inside < own + GHOST, owner * GHOST + inside + (n_dev * own - own),
                  owner * GHOST + inside + (n_dev * (own + GHOST) - own - GHOST)),
    )
    place = jnp.where(pat < 0, -1.0, place)
    first_own = (me_d * own).astype(F32)
    sub8 = lax.broadcasted_iota(jnp.int32, (8, LANES), 0).astype(F32)

    def fill_index(m, carry):
        rolled = pltpu.roll(place, lax.rem(LANES - m, LANES), 1)
        base = pl.multiple_of(m * LANES, LANES)
        for member in range(MEMBERS):
            first = member * n_groups
            column = jnp.broadcast_to(rolled[:, first : first + 1], (slots, LANES))
            if first + n_groups > own:
                column = jnp.where(first + m < own, column, -1.0)
            idxb[pl.ds(base + member * slots, slots), :] = column
        mine = sub8 * n_groups + jnp.asarray(m, jnp.int32).astype(F32)
        mine = jnp.where((sub8 < MEMBERS) & (mine < own), mine + first_own, -1.0)
        idxb[pl.ds(base + MEMBERS * slots, 8), :] = mine
        return carry

    lax.fori_loop(0, n_groups, fill_index, 0, unroll=UNROLL_INDEX)

    code_rows = 16
    adj_rows = own + code_rows

    def adj_block(zz, cc, at=0, size=None):
        size = adj_rows if size is None else size
        return adjg.at[zz, pl.ds(pl.multiple_of(cc * adj_rows + at, 16), size), :]

    adj_load.wait()
    adj_at = pl.ds(pl.multiple_of(code_rows + c * own, 16), own)
    for p in range(points):
        cut = slice(p * objs, (p + 1) * objs)
        high = adj_own[p].astype(BF16)
        adjg[z, adj_at, cut] = high
        adj_low[:, cut] = (adj_own[p] - high.astype(F32)).astype(BF16)
    code_at = pl.ds(pl.multiple_of(c * (2 * own + code_rows), 16), code_rows)
    for j in range(slots // 8):
        cut = slice(8 * j, 8 * j + 8)
        codes = jnp.concatenate([owner[cut], inside[cut]], axis=0)
        adjg[z, code_at, j * LANES : (j + 1) * LANES] = codes.astype(BF16)

    for load in loads:
        load.wait()
    pl.semaphore_wait(barrier, len(greeted))

    piece = own // TURNS
    waiting_ghost = []

    def ghost_at(zz, cc):
        return pl.ds(pl.multiple_of((zz * 2 + cc) * GHOST, GHOST), GHOST)

    def pass_ghost(zz):
        src = block(zz, c, 0, GHOST)
        for to in (0, 1):
            for cc in (c, other):
                device = {"grp": sides[to], "dev": z * 2 + cc}
                at = copies.start(src, ghost.at[to, ghost_at(zz, c), :], device)
                waiting_ghost.append((at, to, zz, cc, device))

    def forward_row(flow, zz, part):
        ref = block(zz, c, part * piece, piece)
        return copies.start(ref, ref, ring[flow])

    def share_row(zz):
        ref = block(zz, c)
        return copies.start(ref, ref, partner), zz

    def part_of(flow, turn):
        return TURNS - 1 - turn if flow else turn

    pieces = {}
    for turn in range(TURNS if far > 1 else TURNS // 2):
        for flow in (0, 1):
            pieces[flow, turn] = forward_row(flow, z, part_of(flow, turn))
    shared = [share_row(z)]
    far_ghost = []
    for to in (0, 1):
        device = {"grp": sides[to], "dev": chip(far) * 2 + c}
        far_ghost.append((copies.start(block(z, c, 0, GHOST), ghost.at[to, ghost_at(z, c), :], device), to, device))
    pass_ghost(z)
    def add_tile(load, base, depth, first=False):
        base = jnp.asarray(base, jnp.int32).astype(F32)

        def body(step, carry):
            at = pl.ds(pl.multiple_of(step * PER_STEP, PER_STEP), PER_STEP)
            relative = idxb[at, :] - base
            parts = []
            for lane in range(0, depth, LANES):
                wide = min(LANES, depth - lane)
                lanes = (lax.broadcasted_iota(jnp.int32, (PER_STEP, wide), 1) + lane).astype(F32)
                parts.append(jnp.where(relative[:, :wide] == lanes, 1.0, 0.0).astype(BF16))
            hot = parts[0] if len(parts) == 1 else jnp.concatenate(parts, axis=1)
            total = jnp.dot(hot, load(), preferred_element_type=F32).astype(BF16)
            near[at, :] = total if first else near[at, :] + total
            return carry

        lax.fori_loop(0, near.shape[0] // PER_STEP, body, 0)

    def chip_tile(zz, first=False):
        add_tile(lambda: pool[zz], zz * (2 * own), 2 * own, first)

    def take_shared(found):
        for at, zz in found:
            copies.arrived(at, block(zz, other), partner)

    def take(hop, turn):
        for flow, zz in ((0, chip(-hop)), (1, chip(hop))):
            if (flow, turn) not in pieces:
                continue
            part = part_of(flow, turn)
            copies.arrived(pieces[flow, turn], block(zz, c, part * piece, piece), ring[flow])
            if hop < far - 1 or (hop == far - 1 and turn < TURNS // 2):
                later[flow, turn] = forward_row(flow, zz, part)
            if hop < far and part == 0:
                pass_ghost(zz)

    adj_first = adj_rows // 2 // 16 * 16
    adj_cut = ((0, adj_first), (adj_first, adj_rows - adj_first))
    adj_sent, adj_shared = {}, []

    def adj_send(flow, zz, hop, turn):
        ref = adj_block(zz, c, *adj_cut[turn ^ flow])
        adj_sent[flow, hop, turn] = copies.start(ref, ref, ring[flow])

    def adj_start(turn):
        if far > 1 or turn == 0:
            for flow in (0, 1):
                adj_send(flow, z, 1, turn)

    def adj_share(zz):
        ref = adj_block(zz, c)
        adj_shared.append((copies.start(ref, ref, partner), zz))

    def adj_take(hop, turn):
        if hop > far:
            return
        for flow, zz in ((0, chip(-hop)), (1, chip(hop))):
            if (flow, hop, turn) in adj_sent:
                copies.arrived(adj_sent[flow, hop, turn], adj_block(zz, c, *adj_cut[turn ^ flow]), ring[flow])
                if hop < far - 1 or (hop == far - 1 and turn == 0):
                    adj_send(flow, zz, hop + 1, turn)
            if hop < far and turn == 1:
                adj_share(zz)
        if hop == far and turn == 0:
            adj_share(chip(hop))

    if far == 1:
        adj_start(0)
    waiting_tiles = [z]
    for hop in range(1, far + 1):
        later = {}
        for turn in range(TURNS // 2):
            take(hop, turn)
        take_shared(shared)
        if hop == far:
            adj_start(1)
            adj_take(1, 0)
            shared = [share_row(chip(hop))]
            break
        chip_tile(waiting_tiles.pop(0), first=hop == 1)
        for turn in range(TURNS // 2, TURNS):
            take(hop, turn)
        pieces = later
        now = [chip(-hop), chip(hop)]
        shared = [share_row(zz) for zz in now]
        if hop == far - 1:
            adj_start(0)
        for zz in waiting_tiles:
            chip_tile(zz)
        waiting_tiles = now

    relayed = []
    for at, to, device in far_ghost:
        ref = ghost.at[to, ghost_at(chip(far), c), :]
        copies.arrived(at, ref, device)
        relayed.append((copies.start(ref, ref, partner), to))
    adj_share(z)
    chip_tile(waiting_tiles[0], first=far == 1)
    adj_take(1, 1)
    for zz in waiting_tiles[1:]:
        chip_tile(zz)
    take_shared(shared)
    chip_tile(chip(far))
    adj_take(2, 0)
    for at, to, zz, cc, device in waiting_ghost:
        copies.arrived(at, ghost.at[to, ghost_at(zz, cc), :], device)
    for at, to in relayed:
        copies.arrived(at, ghost.at[to, ghost_at(chip(far), other), :], partner)
    side_rows = n_dev * GHOST
    add_tile((lambda: ghost[0]), n_dev * own, side_rows)
    adj_take(2, 1)
    add_tile((lambda: ghost[1]), n_dev * own + side_rows, side_rows)

    lane = lax.broadcasted_iota(jnp.int32, (slots, LANES), 1)
    sub = lax.broadcasted_iota(jnp.int32, (slots, LANES), 0)
    ridge = jnp.zeros((slots, LANES), F32)
    for member in range(MEMBERS):
        ridge = jnp.where(lane - member * slots == sub, ridge_share * width, ridge)
    lane8 = lax.broadcasted_iota(jnp.int32, (8, LANES), 1)
    row8 = lax.broadcasted_iota(jnp.int32, (8, LANES), 0)
    own_mask = (lane8 >= row8 * slots) & (lane8 < row8 * slots + slots)

    def make_gram(m, carry):
        tile = near[pl.ds(pl.multiple_of(m * LANES, LANES), LANES), :]
        for p in range(points):
            part = tile[:, p * width : (p + 1) * width]
            full = lax.dot_general(part, part, (((1,), (1,)), ((), ())), preferred_element_type=F32)
            packed = full[:slots]
            for member in range(1, MEMBERS):
                packed = jnp.where(lane >= member * slots, full[member * slots : (member + 1) * slots], packed)
            at = (p * 32 + m) * 32
            gram[pl.ds(pl.multiple_of(at, 32), slots), :] = packed + ridge
            target = jnp.sum(jnp.where(own_mask, full[MEMBERS * slots :], 0.0), axis=0, keepdims=True)
            gram[pl.ds(pl.multiple_of(at + slots, 8), 8), :] = jnp.broadcast_to(target, (8, LANES))
        return carry

    lax.fori_loop(0, n_groups // 2, make_gram, 0, unroll=UNROLL_GRAM)
    adj_take(3, 0)
    lax.fori_loop(n_groups // 2, n_groups, make_gram, 0, unroll=UNROLL_GRAM)
    adj_take(3, 1)

    for i in range(slots + 1):
        turned = jnp.transpose(gram[pl.ds(i, 64, stride=32), :])
        mat[i, :, :, 0:64] = turned[: MEMBERS * slots].reshape(MEMBERS, slots, 64)

    for j0 in range(0, slots, 8):
        span = slots - j0
        at_slot = lax.broadcasted_iota(jnp.int32, (MEMBERS, span, LANES), 1) + j0

        def eliminate(step, carry):
            col = step + j0
            pivot_row = mat[col, :, j0:slots, :]
            inverse = 1.0 / mat[col, :, pl.ds(col, 1), :]
            beyond = at_slot > col
            factors = jnp.where(beyond, pivot_row * inverse, 0.0)
            for i in range(j0, slots):
                block_at = i // 8 * 8
                mat[i, :, block_at:slots, :] = (
                    mat[i, :, block_at:slots, :] - factors[:, i - j0 : i - j0 + 1, :] * pivot_row[:, block_at - j0 :, :]
                )
            rhs = mat[slots, :, pl.ds(col, 1), :]
            mat[slots, :, j0:slots, :] = mat[slots, :, j0:slots, :] - rhs * factors
            return carry

        lax.fori_loop(0, 8, eliminate, 0)
    adj_take(4, 0)
    at_slot = lax.broadcasted_iota(jnp.int32, (MEMBERS, slots, LANES), 1)
    solved = jnp.zeros((MEMBERS, slots, LANES), F32)
    for col in range(slots - 1, -1, -1):
        line = mat[col]
        inverse = 1.0 / line[:, col : col + 1, :]
        scaled = jnp.where(at_slot > col, line * inverse, 0.0)
        known = jnp.sum(scaled * solved, axis=1, keepdims=True)
        value = mat[slots, :, col : col + 1, :] * inverse - known
        solved = jnp.where(at_slot == col, value, solved)

    coef_rows = points * slots

    def coef_block(zz, cc):
        return coefg.at[zz, pl.ds(pl.multiple_of(cc * coef_rows, 8), coef_rows), :]

    for p in range(points):
        coeff = jnp.zeros((slots, LANES), F32)
        for member in range(MEMBERS):
            first = member * n_groups
            rolled = pltpu.roll(solved[member], (first - 32 * p) % LANES, 1)
            coeff = jnp.where((lane >= first) & (lane < first + n_groups), rolled, coeff)
        coefg[z, pl.ds(pl.multiple_of(c * coef_rows + p * slots, 8), slots), :] = coeff

    coef_sent = {}
    for hop in range(far, 0, -1):
        for step in (hop, -hop) if hop < far else (hop,):
            ref = coef_block(z, c)
            coef_sent[step] = copies.start(ref, ref, peer(step))

    def coef_share(zz):
        ref = coef_block(zz, c)
        return copies.start(ref, ref, partner), zz

    shared = [coef_share(z)]
    me_f = me_d.astype(F32)
    entry = lax.broadcasted_iota(jnp.int32, (ext, LANES), 0).astype(F32)

    def make_table(zz, cc):
        code_at = pl.multiple_of(cc * (2 * own + code_rows), 16)
        picked = []
        for j in range(slots // 8):
            codes = adjg[zz, pl.ds(code_at, code_rows), j * LANES : (j + 1) * LANES].astype(F32)
            picked.append(jnp.where(codes[:8] == me_f, codes[8:], -1.0))
        weights = coefg[zz, pl.ds(pl.multiple_of(cc * coef_rows, 8), coef_rows), :]
        tables = [jnp.zeros((ext, LANES), F32) for _ in range(points)]
        for k in range(slots):
            match = picked[k // 8][k % 8 : k % 8 + 1] == entry
            for p in range(points):
                row = p * slots + k
                tables[p] = tables[p] + jnp.where(match, weights[row : row + 1], 0.0)
        at = pl.ds(pl.multiple_of((zz * 2 + cc) * LANES, LANES), LANES)
        for p in range(points):
            high = tables[p].astype(BF16)
            tall[p, 0:ext, at] = high
            tall[p, ext : 2 * ext, at] = (tables[p] - high.astype(F32)).astype(BF16)

    def table_loop(hop, cc, count):
        def body(i, carry):
            make_table(jnp.where(i == 0, chip(-hop), chip(hop)), cc)
            return carry

        lax.fori_loop(0, count, body, 0)

    def take_coef(found):
        for at, zz in found:
            copies.arrived(at, coef_block(zz, other), partner)

    make_table(z, c)
    take_coef(shared)
    adj_take(4, 1)
    for hop in range(5, far + 1):
        adj_take(hop, 0)
        adj_take(hop, 1)
    for at, zz in adj_shared:
        copies.arrived(at, adj_block(zz, other), partner)
    make_table(z, other)
    own_lanes = pl.ds(pl.multiple_of(me_d * LANES, LANES), LANES)

    def multiply(zz, first=False):
        lanes = pl.ds(pl.multiple_of(zz * 2 * LANES, 2 * LANES), 2 * LANES)
        for p in range(points):
            cut = slice(p * objs, (p + 1) * objs)
            product = jnp.dot(tall[p, :, lanes], adjg[zz, code_rows : code_rows + 2 * own, cut],
                              preferred_element_type=F32)
            product = product[:ext] + product[ext:]
            if first:
                acc[p] = product + jnp.dot(tall[p, :ext, own_lanes], adj_low[:, cut], preferred_element_type=F32)
            else:
                acc[p] = acc[p] + product

    multiply(z, first=True)
    for hop in range(1, far + 1):
        shared = []
        for step in (-hop, hop) if hop < far else (hop,):
            copies.arrived(coef_sent[-step if hop < far else step], coef_block(chip(step), c), peer(step))
            shared.append(coef_share(chip(step)))
        table_loop(hop, c, len(shared))
        take_coef(shared)
        table_loop(hop, other, len(shared))
        for _, zz in shared:
            multiply(zz)

    low_rows, high_rows = acc.at[:, own : own + GHOST, :], acc.at[:, own + GHOST : ext, :]
    from_above = copies.start(low_rows, back.at[0], {"grp": below})
    from_below = copies.start(high_rows, back.at[1], {"grp": above})
    out_ref[...] = adj_own[...] - acc[:, :own, :]
    copies.arrived(from_above, back.at[0], {"grp": below})
    copies.arrived(from_below, back.at[1], {"grp": above})
    out_ref[:, :GHOST, :] = out_ref[:, :GHOST, :] - (back[0] + back[1])
    copies.finish()


def local(rows, adj_rhs, pattern, lengths):
    points, own, width = rows.shape
    slots = pattern.shape[1]
    objs = adj_rhs.shape[2]
    n_grp, n_dev = lax.axis_size("grp"), lax.axis_size("dev")
    n_z = n_dev // 2
    n_groups = -(-own // MEMBERS)
    ext = own + 2 * GHOST
    n_copies = 120
    vmem = pl.BlockSpec(memory_space=pltpu.VMEM)
    anywhere = pl.BlockSpec(memory_space=pl.ANY)
    return pl.pallas_call(
        functools.partial(kernel, (n_grp, n_dev, points, own, width, slots, objs)),
        out_shape=jax.ShapeDtypeStruct(adj_rhs.shape, F32),
        in_specs=[anywhere, anywhere, vmem, vmem],
        out_specs=vmem,
        scratch_shapes=[
            pltpu.VMEM((n_z, 2 * own, points * width), BF16),
            pltpu.VMEM((2, n_dev * GHOST, points * width), BF16),
            pltpu.VMEM((n_groups * LANES, LANES), F32),
            pltpu.VMEM((n_groups * LANES, points * width), BF16),
            pltpu.VMEM((n_z, 2 * own + 32, points * objs), BF16),
            pltpu.VMEM((own, points * objs), BF16),
            pltpu.VMEM((n_z, 2 * points * slots, LANES), F32),
            pltpu.VMEM((64 * 32, LANES), F32),
            pltpu.VMEM((slots + 1, MEMBERS, slots, LANES), F32),
            pltpu.VMEM((points, 2 * ext, n_dev * LANES), BF16),
            pltpu.VMEM((points, own, objs), F32),
            pltpu.VMEM((points, ext, objs), F32),
            pltpu.VMEM((2, points, GHOST, objs), F32),
            pltpu.SemaphoreType.DMA((n_copies,)),
            pltpu.SemaphoreType.DMA((n_copies,)),
            pltpu.SemaphoreType.DMA((points + 1,)),
        ],
        compiler_params=pltpu.CompilerParams(
            collective_id=0, has_side_effects=True, vmem_limit_bytes=48 * 1024 * 1024
        ),
    )(rows, adj_rhs, pattern, lengths.reshape(1, own))


def solution(mesh):
    placed = (
        P(None, ("grp", "dev"), None),
        P(None, ("grp", "dev"), None),
        P(("grp", "dev"), None),
        P(("grp", "dev")),
    )
    return jax.shard_map(
        local, mesh=mesh, in_specs=placed, out_specs=P(None, ("grp", "dev"), None), check_vma=False
    )
```

```python
import functools

import jax
import jax.numpy as jnp
from jax import lax
from jax.experimental import pallas as pl
from jax.experimental.pallas import tpu as pltpu
from jax.sharding import PartitionSpec as P

GHOST = 16
ridge_share = 0.25

MESH = pl.DeviceIdType.MESH
F32 = jnp.float32
BF16 = jnp.bfloat16
MEMBERS = 5
LANES = 128
PER_STEP = 3328
UNROLL_INDEX = 13
TURNS = 4
UNROLL_GRAM = 13


class Copies:
    def __init__(self, send, recv):
        self.send, self.recv, self.started, self.gone = send, recv, [], set()

    def start(self, src, dst, device):
        at = len(self.started)
        copy = pltpu.make_async_remote_copy(
            src_ref=src, dst_ref=dst, send_sem=self.send.at[at], recv_sem=self.recv.at[at],
            device_id=device, device_id_type=MESH,
        )
        copy.start()
        self.started.append(copy)
        return at

    def arrived(self, at, dst, device):
        pltpu.make_async_remote_copy(
            src_ref=dst, dst_ref=dst, send_sem=self.send.at[at], recv_sem=self.recv.at[at],
            device_id=device, device_id_type=MESH,
        ).wait_recv()

    def left(self, at):
        self.started[at].wait_send()
        self.gone.add(at)

    def finish(self):
        for at, copy in enumerate(self.started):
            if at not in self.gone:
                copy.wait_send()


def kernel(dims, rows_ref, adj_ref, pat_ref, len_ref, out_ref, pool, ghost, idxb, near, adjg, adj_low, coefg, gram, mat,
           tall, adj_own, acc, back, send_sems, recv_sems, load_sems):
    n_grp, n_dev, points, own, width, slots, objs = dims
    n_z = n_dev // 2
    far = n_z // 2
    ext = own + 2 * GHOST
    n_groups = near.shape[0] // LANES
    me_g, me_d = lax.axis_index("grp"), lax.axis_index("dev")
    z, c = lax.div(me_d, 2), lax.rem(me_d, 2)
    other = 1 - c

    def chip(step):
        return lax.rem(z + step + n_z, n_z)

    def peer(step):
        return {"dev": chip(step) * 2 + c}

    right, left = peer(1), peer(-1)
    partner = {"dev": z * 2 + other}
    above, below = lax.rem(me_g + 1, n_grp), lax.rem(me_g + n_grp - 1, n_grp)
    sides = (above, below)
    ring = (right, left)
    copies = Copies(send_sems, recv_sems)

    barrier = pltpu.get_barrier_semaphore()
    greeted = [peer(step) for step in range(1, n_z)] + [partner]
    for side in sides:
        greeted += [{"grp": side}, {"grp": side, "dev": z * 2 + other}, {"grp": side, "dev": chip(far) * 2 + c}]
    for device in greeted:
        pl.semaphore_signal(barrier, inc=1, device_id=device, device_id_type=MESH)

    def block(zz, cc, at=0, size=None):
        size = own if size is None else size
        return pool.at[zz, pl.ds(pl.multiple_of(cc * own + at, 16), size), :]

    mine_at = pl.ds(pl.multiple_of(c * own, own), own)
    loads = [
        pltpu.make_async_copy(rows_ref.at[p], pool.at[z, mine_at, pl.ds(p * width, width)], load_sems.at[p])
        for p in range(points)
    ]
    adj_load = pltpu.make_async_copy(adj_ref, adj_own, load_sems.at[points])
    for load in loads:
        load.start()
    adj_load.start()
    pat = pat_ref[...].astype(F32)
    pat = jnp.transpose(jnp.concatenate([pat, jnp.zeros((own, LANES - slots), F32)], axis=1))[:slots]
    slot_of = lax.broadcasted_iota(jnp.int32, (slots, own), 0)
    pat = jnp.where(slot_of < len_ref[...], pat, -1.0)
    owner = jnp.floor((pat + 0.5) * (1.0 / ext))
    inside = pat - owner * ext
    place = jnp.where(
        inside < own,
        owner * own + inside,
        jnp.where(inside < own + GHOST, owner * GHOST + inside + (n_dev * own - own),
                  owner * GHOST + inside + (n_dev * (own + GHOST) - own - GHOST)),
    )
    place = jnp.where(pat < 0, -1.0, place)
    first_own = (me_d * own).astype(F32)
    sub8 = lax.broadcasted_iota(jnp.int32, (8, LANES), 0).astype(F32)

    def fill_index(m, carry):
        rolled = pltpu.roll(place, lax.rem(LANES - m, LANES), 1)
        base = pl.multiple_of(m * LANES, LANES)
        for member in range(MEMBERS):
            first = member * n_groups
            column = jnp.broadcast_to(rolled[:, first : first + 1], (slots, LANES))
            if first + n_groups > own:
                column = jnp.where(first + m < own, column, -1.0)
            idxb[pl.ds(base + member * slots, slots), :] = column
        mine = sub8 * n_groups + jnp.asarray(m, jnp.int32).astype(F32)
        mine = jnp.where((sub8 < MEMBERS) & (mine < own), mine + first_own, -1.0)
        idxb[pl.ds(base + MEMBERS * slots, 8), :] = mine
        return carry

    lax.fori_loop(0, n_groups, fill_index, 0, unroll=UNROLL_INDEX)

    code_rows = 16
    adj_rows = own + code_rows

    def adj_block(zz, cc, at=0, size=None):
        size = adj_rows if size is None else size
        return adjg.at[zz, pl.ds(pl.multiple_of(cc * adj_rows + at, 16), size), :]

    adj_load.wait()
    adj_at = pl.ds(pl.multiple_of(code_rows + c * own, 16), own)
    for p in range(points):
        cut = slice(p * objs, (p + 1) * objs)
        high = adj_own[p].astype(BF16)
        adjg[z, adj_at, cut] = high
        adj_low[:, cut] = (adj_own[p] - high.astype(F32)).astype(BF16)
    code_at = pl.ds(pl.multiple_of(c * (2 * own + code_rows), 16), code_rows)
    for j in range(slots // 8):
        cut = slice(8 * j, 8 * j + 8)
        codes = jnp.concatenate([owner[cut], inside[cut]], axis=0)
        adjg[z, code_at, j * LANES : (j + 1) * LANES] = codes.astype(BF16)

    for load in loads:
        load.wait()
    pl.semaphore_wait(barrier, len(greeted))

    piece = own // TURNS
    waiting_ghost = []

    def ghost_at(zz, cc):
        return pl.ds(pl.multiple_of((zz * 2 + cc) * GHOST, GHOST), GHOST)

    def pass_ghost(zz):
        src = block(zz, c, 0, GHOST)
        for to in (0, 1):
            for cc in (c, other):
                device = {"grp": sides[to], "dev": z * 2 + cc}
                at = copies.start(src, ghost.at[to, ghost_at(zz, c), :], device)
                waiting_ghost.append((at, to, zz, cc, device))

    def forward_row(flow, zz, part):
        ref = block(zz, c, part * piece, piece)
        return copies.start(ref, ref, ring[flow])

    def share_row(zz):
        ref = block(zz, c)
        return copies.start(ref, ref, partner), zz

    def part_of(flow, turn):
        return (TURNS - turn) % TURNS if flow else turn

    def goes_far(flow, part):
        return (part >= TURNS // 2) == (flow == 1)

    pieces = {}
    for turn in range(TURNS):
        for flow in (0, 1):
            if far > 1 or goes_far(flow, part_of(flow, turn)):
                pieces[flow, turn] = forward_row(flow, z, part_of(flow, turn))
    shared = [share_row(z)]
    far_ghost = []
    for to in (0, 1):
        device = {"grp": sides[to], "dev": chip(far) * 2 + c}
        far_ghost.append((copies.start(block(z, c, 0, GHOST), ghost.at[to, ghost_at(z, c), :], device), to, device))
    pass_ghost(z)
    def add_tile(load, base, depth, first=False):
        base = jnp.asarray(base, jnp.int32).astype(F32)

        def body(step, carry):
            at = pl.ds(pl.multiple_of(step * PER_STEP, PER_STEP), PER_STEP)
            relative = idxb[at, :] - base
            parts = []
            for lane in range(0, depth, LANES):
                wide = min(LANES, depth - lane)
                lanes = (lax.broadcasted_iota(jnp.int32, (PER_STEP, wide), 1) + lane).astype(F32)
                parts.append(jnp.where(relative[:, :wide] == lanes, 1.0, 0.0).astype(BF16))
            hot = parts[0] if len(parts) == 1 else jnp.concatenate(parts, axis=1)
            total = jnp.dot(hot, load(), preferred_element_type=F32).astype(BF16)
            near[at, :] = total if first else near[at, :] + total
            return carry

        lax.fori_loop(0, near.shape[0] // PER_STEP, body, 0)

    def chip_tile(zz, first=False):
        add_tile(lambda: pool[zz], zz * (2 * own), 2 * own, first)

    def take_shared(found):
        for at, zz in found:
            copies.arrived(at, block(zz, other), partner)

    def take(hop, turn):
        for flow, zz in ((0, chip(-hop)), (1, chip(hop))):
            if (flow, turn) not in pieces:
                continue
            part = part_of(flow, turn)
            copies.arrived(pieces[flow, turn], block(zz, c, part * piece, piece), ring[flow])
            if hop < far - 1 or (hop == far - 1 and goes_far(flow, part)):
                later[flow, turn] = forward_row(flow, zz, part)
            if hop < far and part == 0:
                pass_ghost(zz)

    adj_first = adj_rows // 2 // 16 * 16
    adj_cut = ((0, adj_first), (adj_first, adj_rows - adj_first))
    adj_sent, adj_shared = {}, {hop: [] for hop in range(far + 1)}

    def adj_send(flow, zz, hop, turn):
        ref = adj_block(zz, c, *adj_cut[turn ^ flow])
        adj_sent[flow, hop, turn] = copies.start(ref, ref, ring[flow])

    def adj_start(turn):
        if far > 1 or turn == 0:
            for flow in (0, 1):
                adj_send(flow, z, 1, turn)

    def adj_share(hop, zz):
        ref = adj_block(zz, c)
        adj_shared[hop].append((copies.start(ref, ref, partner), zz))

    def adj_take(hop, turn):
        if hop > far:
            return
        for flow, zz in ((0, chip(-hop)), (1, chip(hop))):
            if (flow, hop, turn) in adj_sent:
                copies.arrived(adj_sent[flow, hop, turn], adj_block(zz, c, *adj_cut[turn ^ flow]), ring[flow])
                if hop < far - 1 or (hop == far - 1 and turn == 0):
                    adj_send(flow, zz, hop + 1, turn)
            if hop < far and turn == 1:
                adj_share(hop, zz)
        if hop == far and turn == 0:
            adj_share(hop, chip(hop))

    if far <= 2:
        adj_start(0)
    waiting_tiles = [z]
    for hop in range(1, far):
        later = {}
        for turn in range(TURNS // 2):
            take(hop, turn)
        take_shared(shared)
        chip_tile(waiting_tiles.pop(0), first=hop == 1)
        for turn in range(TURNS // 2, TURNS):
            take(hop, turn)
        pieces = later
        now = [chip(-hop), chip(hop)]
        shared = [share_row(zz) for zz in now]
        if hop == far - 2:
            adj_start(0)
        if hop == far - 1:
            adj_take(1, 0)
            adj_start(1)
        for zz in waiting_tiles:
            chip_tile(zz)
        waiting_tiles = now
    relayed = []
    for at, to, device in far_ghost:
        ref = ghost.at[to, ghost_at(chip(far), c), :]
        copies.arrived(at, ref, device)
        relayed.append((copies.start(ref, ref, partner), to))
    adj_share(0, z)
    take_shared(shared)
    chip_tile(waiting_tiles[0], first=far == 1)
    for zz in waiting_tiles[1:]:
        chip_tile(zz)
    for turn in range(TURNS):
        take(far, turn)
    shared = [share_row(chip(far))]
    if far == 1:
        adj_take(1, 0)
    adj_take(1, 1)
    adj_take(2, 0)
    for at, to, zz, cc, device in waiting_ghost:
        copies.arrived(at, ghost.at[to, ghost_at(zz, cc), :], device)
    for at, to in relayed:
        copies.arrived(at, ghost.at[to, ghost_at(chip(far), other), :], partner)
    side_rows = n_dev * GHOST
    add_tile((lambda: ghost[0]), n_dev * own, side_rows)
    take_shared(shared)
    chip_tile(chip(far))
    adj_take(2, 1)
    add_tile((lambda: ghost[1]), n_dev * own + side_rows, side_rows)
    adj_take(3, 0)

    lane = lax.broadcasted_iota(jnp.int32, (slots, LANES), 1)
    sub = lax.broadcasted_iota(jnp.int32, (slots, LANES), 0)
    ridge = jnp.zeros((slots, LANES), F32)
    for member in range(MEMBERS):
        ridge = jnp.where(lane - member * slots == sub, ridge_share * width, ridge)
    lane8 = lax.broadcasted_iota(jnp.int32, (8, LANES), 1)
    row8 = lax.broadcasted_iota(jnp.int32, (8, LANES), 0)
    own_mask = (lane8 >= row8 * slots) & (lane8 < row8 * slots + slots)

    def make_gram(m, carry):
        tile = near[pl.ds(pl.multiple_of(m * LANES, LANES), LANES), :]
        for p in range(points):
            part = tile[:, p * width : (p + 1) * width]
            full = lax.dot_general(part, part, (((1,), (1,)), ((), ())), preferred_element_type=F32)
            packed = full[:slots]
            for member in range(1, MEMBERS):
                packed = jnp.where(lane >= member * slots, full[member * slots : (member + 1) * slots], packed)
            at = (p * 32 + m) * 32
            gram[pl.ds(pl.multiple_of(at, 32), slots), :] = packed + ridge
            target = jnp.sum(jnp.where(own_mask, full[MEMBERS * slots :], 0.0), axis=0, keepdims=True)
            gram[pl.ds(pl.multiple_of(at + slots, 8), 8), :] = jnp.broadcast_to(target, (8, LANES))
        return carry

    lax.fori_loop(0, n_groups // 2, make_gram, 0, unroll=UNROLL_GRAM)
    lax.fori_loop(n_groups // 2, n_groups, make_gram, 0, unroll=UNROLL_GRAM)
    adj_take(3, 1)

    for i in range(slots + 1):
        turned = jnp.transpose(gram[pl.ds(i, 64, stride=32), :])
        mat[i, :, :, 0:64] = turned[: MEMBERS * slots].reshape(MEMBERS, slots, 64)

    for j0 in range(0, slots, 8):
        span = slots - j0
        at_slot = lax.broadcasted_iota(jnp.int32, (MEMBERS, span, LANES), 1) + j0

        def eliminate(step, carry):
            col = step + j0
            pivot_row = mat[col, :, j0:slots, :]
            inverse = 1.0 / mat[col, :, pl.ds(col, 1), :]
            beyond = at_slot > col
            factors = jnp.where(beyond, pivot_row * inverse, 0.0)
            for i in range(j0, slots):
                block_at = i // 8 * 8
                mat[i, :, block_at:slots, :] = (
                    mat[i, :, block_at:slots, :] - factors[:, i - j0 : i - j0 + 1, :] * pivot_row[:, block_at - j0 :, :]
                )
            rhs = mat[slots, :, pl.ds(col, 1), :]
            mat[slots, :, j0:slots, :] = mat[slots, :, j0:slots, :] - rhs * factors
            return carry

        lax.fori_loop(0, 8, eliminate, 0)
    at_slot = lax.broadcasted_iota(jnp.int32, (MEMBERS, slots, LANES), 1)
    solved = jnp.zeros((MEMBERS, slots, LANES), F32)
    for col in range(slots - 1, -1, -1):
        line = mat[col]
        inverse = 1.0 / line[:, col : col + 1, :]
        scaled = jnp.where(at_slot > col, line * inverse, 0.0)
        known = jnp.sum(scaled * solved, axis=1, keepdims=True)
        value = mat[slots, :, col : col + 1, :] * inverse - known
        solved = jnp.where(at_slot == col, value, solved)

    coef_rows = points * slots

    def coef_block(zz, cc):
        return coefg.at[zz, pl.ds(pl.multiple_of(cc * coef_rows, 8), coef_rows), :]

    for p in range(points):
        coeff = jnp.zeros((slots, LANES), F32)
        for member in range(MEMBERS):
            first = member * n_groups
            rolled = pltpu.roll(solved[member], (first - 32 * p) % LANES, 1)
            coeff = jnp.where((lane >= first) & (lane < first + n_groups), rolled, coeff)
        coefg[z, pl.ds(pl.multiple_of(c * coef_rows + p * slots, 8), slots), :] = coeff

    coef_sent = {}
    for hop in sorted(range(1, far + 1), key=lambda hop: hop):
        for step in (hop, -hop) if hop < far else (hop,):
            ref = coef_block(z, c)
            coef_sent[step] = copies.start(ref, ref, peer(step))

    def coef_share(zz):
        ref = coef_block(zz, c)
        return copies.start(ref, ref, partner), zz

    shared = [coef_share(z)]
    me_f = me_d.astype(F32)
    entry = lax.broadcasted_iota(jnp.int32, (ext, LANES), 0).astype(F32)

    def make_table(zz, cc):
        code_at = pl.multiple_of(cc * (2 * own + code_rows), 16)
        picked = []
        for j in range(slots // 8):
            codes = adjg[zz, pl.ds(code_at, code_rows), j * LANES : (j + 1) * LANES].astype(F32)
            picked.append(jnp.where(codes[:8] == me_f, codes[8:], -1.0))
        weights = coefg[zz, pl.ds(pl.multiple_of(cc * coef_rows, 8), coef_rows), :]
        tables = [jnp.zeros((ext, LANES), F32) for _ in range(points)]
        for k in range(slots):
            match = picked[k // 8][k % 8 : k % 8 + 1] == entry
            for p in range(points):
                row = p * slots + k
                tables[p] = tables[p] + jnp.where(match, weights[row : row + 1], 0.0)
        at = pl.ds(pl.multiple_of((zz * 2 + cc) * LANES, LANES), LANES)
        for p in range(points):
            high = tables[p].astype(BF16)
            tall[p, 0:ext, at] = high
            tall[p, ext : 2 * ext, at] = (tables[p] - high.astype(F32)).astype(BF16)

    def table_loop(hop, cc, count):
        def body(i, carry):
            make_table(jnp.where(i == 0, chip(-hop), chip(hop)), cc)
            return carry

        lax.fori_loop(0, count, body, 0)

    def take_coef(found):
        for at, zz in found:
            copies.arrived(at, coef_block(zz, other), partner)

    make_table(z, c)
    take_coef(shared)

    def take_adj(hop):
        for at, zz in adj_shared[hop]:
            copies.arrived(at, adj_block(zz, other), partner)

    take_adj(0)
    make_table(z, other)
    own_lanes = pl.ds(pl.multiple_of(me_d * LANES, LANES), LANES)

    def multiply(zz, first=False):
        lanes = pl.ds(pl.multiple_of(zz * 2 * LANES, 2 * LANES), 2 * LANES)
        for p in range(points):
            cut = slice(p * objs, (p + 1) * objs)
            product = jnp.dot(tall[p, :, lanes], adjg[zz, code_rows : code_rows + 2 * own, cut],
                              preferred_element_type=F32)
            product = product[:ext] + product[ext:]
            if first:
                acc[p] = product + jnp.dot(tall[p, :ext, own_lanes], adj_low[:, cut], preferred_element_type=F32)
            else:
                acc[p] = acc[p] + product

    multiply(z, first=True)

    def second_half(hop, found):
        take_coef(found)
        take_adj(hop)
        table_loop(hop, other, len(found))
        for _, zz in found:
            multiply(zz)

    before = []
    for hop in range(1, far + 1):
        shared = []
        for step in (-hop, hop) if hop < far else (hop,):
            copies.arrived(coef_sent[-step if hop < far else step], coef_block(chip(step), c), peer(step))
            shared.append(coef_share(chip(step)))
        if hop == 4:
            adj_take(4, 0)
        table_loop(hop, c, len(shared))
        if before:
            second_half(hop - 1, before)
        before = shared
    second_half(far, before)

    low_rows, high_rows = acc.at[:, own : own + GHOST, :], acc.at[:, own + GHOST : ext, :]
    from_above = copies.start(low_rows, back.at[0], {"grp": below})
    from_below = copies.start(high_rows, back.at[1], {"grp": above})
    out_ref[...] = adj_own[...] - acc[:, :own, :]
    copies.arrived(from_above, back.at[0], {"grp": below})
    copies.arrived(from_below, back.at[1], {"grp": above})
    out_ref[:, :GHOST, :] = out_ref[:, :GHOST, :] - (back[0] + back[1])
    copies.finish()


def local(rows, adj_rhs, pattern, lengths):
    points, own, width = rows.shape
    slots = pattern.shape[1]
    objs = adj_rhs.shape[2]
    n_grp, n_dev = lax.axis_size("grp"), lax.axis_size("dev")
    n_z = n_dev // 2
    n_groups = -(-own // MEMBERS)
    ext = own + 2 * GHOST
    n_copies = 120
    vmem = pl.BlockSpec(memory_space=pltpu.VMEM)
    anywhere = pl.BlockSpec(memory_space=pl.ANY)
    return pl.pallas_call(
        functools.partial(kernel, (n_grp, n_dev, points, own, width, slots, objs)),
        out_shape=jax.ShapeDtypeStruct(adj_rhs.shape, F32),
        in_specs=[anywhere, anywhere, vmem, vmem],
        out_specs=vmem,
        scratch_shapes=[
            pltpu.VMEM((n_z, 2 * own, points * width), BF16),
            pltpu.VMEM((2, n_dev * GHOST, points * width), BF16),
            pltpu.VMEM((n_groups * LANES, LANES), F32),
            pltpu.VMEM((n_groups * LANES, points * width), BF16),
            pltpu.VMEM((n_z, 2 * own + 32, points * objs), BF16),
            pltpu.VMEM((own, points * objs), BF16),
            pltpu.VMEM((n_z, 2 * points * slots, LANES), F32),
            pltpu.VMEM((64 * 32, LANES), F32),
            pltpu.VMEM((slots + 1, MEMBERS, slots, LANES), F32),
            pltpu.VMEM((points, 2 * ext, n_dev * LANES), BF16),
            pltpu.VMEM((points, own, objs), F32),
            pltpu.VMEM((points, ext, objs), F32),
            pltpu.VMEM((2, points, GHOST, objs), F32),
            pltpu.SemaphoreType.DMA((n_copies,)),
            pltpu.SemaphoreType.DMA((n_copies,)),
            pltpu.SemaphoreType.DMA((points + 1,)),
        ],
        compiler_params=pltpu.CompilerParams(
            collective_id=0, has_side_effects=True, vmem_limit_bytes=48 * 1024 * 1024
        ),
    )(rows, adj_rhs, pattern, lengths.reshape(1, own))


def solution(mesh):
    placed = (
        P(None, ("grp", "dev"), None),
        P(None, ("grp", "dev"), None),
        P(("grp", "dev"), None),
        P(("grp", "dev")),
    )
    return jax.shard_map(
        local, mesh=mesh, in_specs=placed, out_specs=P(None, ("grp", "dev"), None), check_vma=False
    )
```

```python
import functools

import jax
import jax.numpy as jnp
from jax import lax
from jax.experimental import pallas as pl
from jax.experimental.pallas import tpu as pltpu
from jax.sharding import PartitionSpec as P

GHOST = 16
ridge_share = 0.25

MESH = pl.DeviceIdType.MESH
F32 = jnp.float32
BF16 = jnp.bfloat16
MEMBERS = 5
LANES = 128
PER_STEP = 3328
UNROLL_INDEX = 13
TURNS = 4
UNROLL_GRAM = 13


class Copies:
    def __init__(self, send, recv):
        self.send, self.recv, self.started, self.gone = send, recv, [], set()

    def start(self, src, dst, device):
        at = len(self.started)
        copy = pltpu.make_async_remote_copy(
            src_ref=src, dst_ref=dst, send_sem=self.send.at[at], recv_sem=self.recv.at[at],
            device_id=device, device_id_type=MESH,
        )
        copy.start()
        self.started.append(copy)
        return at

    def arrived(self, at, dst, device):
        pltpu.make_async_remote_copy(
            src_ref=dst, dst_ref=dst, send_sem=self.send.at[at], recv_sem=self.recv.at[at],
            device_id=device, device_id_type=MESH,
        ).wait_recv()

    def left(self, at):
        self.started[at].wait_send()
        self.gone.add(at)

    def finish(self):
        for at, copy in enumerate(self.started):
            if at not in self.gone:
                copy.wait_send()


def kernel(dims, rows_ref, adj_ref, pat_ref, len_ref, out_ref, pool, ghost, idxb, near, adjg, adj_low, coefg, gram, mat,
           tall, adj_own, acc, back, send_sems, recv_sems, load_sems):
    n_grp, n_dev, points, own, width, slots, objs = dims
    n_z = n_dev // 2
    far = n_z // 2
    ext = own + 2 * GHOST
    n_groups = near.shape[0] // LANES
    me_g, me_d = lax.axis_index("grp"), lax.axis_index("dev")
    z, c = lax.div(me_d, 2), lax.rem(me_d, 2)
    other = 1 - c

    def chip(step):
        return lax.rem(z + step + n_z, n_z)

    def peer(step):
        return {"dev": chip(step) * 2 + c}

    right, left = peer(1), peer(-1)
    partner = {"dev": z * 2 + other}
    above, below = lax.rem(me_g + 1, n_grp), lax.rem(me_g + n_grp - 1, n_grp)
    sides = (above, below)
    ring = (right, left)
    copies = Copies(send_sems, recv_sems)

    barrier = pltpu.get_barrier_semaphore()
    greeted = [peer(step) for step in range(1, n_z)] + [partner]
    for side in sides:
        greeted += [{"grp": side}, {"grp": side, "dev": z * 2 + other}, {"grp": side, "dev": chip(far) * 2 + c}]
    for device in greeted:
        pl.semaphore_signal(barrier, inc=1, device_id=device, device_id_type=MESH)

    def block(zz, cc, at=0, size=None):
        size = own if size is None else size
        return pool.at[zz, pl.ds(pl.multiple_of(cc * own + at, 16), size), :]

    mine_at = pl.ds(pl.multiple_of(c * own, own), own)
    loads = [
        pltpu.make_async_copy(rows_ref.at[p], pool.at[z, mine_at, pl.ds(p * width, width)], load_sems.at[p])
        for p in range(points)
    ]
    adj_load = pltpu.make_async_copy(adj_ref, adj_own, load_sems.at[points])
    for load in loads:
        load.start()
    adj_load.start()
    pat = pat_ref[...].astype(F32)
    pat = jnp.transpose(jnp.concatenate([pat, jnp.zeros((own, LANES - slots), F32)], axis=1))[:slots]
    slot_of = lax.broadcasted_iota(jnp.int32, (slots, own), 0)
    pat = jnp.where(slot_of < len_ref[...], pat, -1.0)
    owner = jnp.floor((pat + 0.5) * (1.0 / ext))
    inside = pat - owner * ext
    place = jnp.where(
        inside < own,
        owner * own + inside,
        jnp.where(inside < own + GHOST, owner * GHOST + inside + (n_dev * own - own),
                  owner * GHOST + inside + (n_dev * (own + GHOST) - own - GHOST)),
    )
    place = jnp.where(pat < 0, -1.0, place)
    first_own = (me_d * own).astype(F32)
    sub8 = lax.broadcasted_iota(jnp.int32, (8, LANES), 0).astype(F32)

    def fill_index(m, carry):
        rolled = pltpu.roll(place, lax.rem(LANES - m, LANES), 1)
        base = pl.multiple_of(m * LANES, LANES)
        for member in range(MEMBERS):
            first = member * n_groups
            column = jnp.broadcast_to(rolled[:, first : first + 1], (slots, LANES))
            if first + n_groups > own:
                column = jnp.where(first + m < own, column, -1.0)
            idxb[pl.ds(base + member * slots, slots), :] = column
        mine = sub8 * n_groups + jnp.asarray(m, jnp.int32).astype(F32)
        mine = jnp.where((sub8 < MEMBERS) & (mine < own), mine + first_own, -1.0)
        idxb[pl.ds(base + MEMBERS * slots, 8), :] = mine
        return carry

    lax.fori_loop(0, n_groups, fill_index, 0, unroll=UNROLL_INDEX)

    code_rows = 16
    adj_rows = own + code_rows

    def adj_block(zz, cc, at=0, size=None):
        size = adj_rows if size is None else size
        return adjg.at[zz, pl.ds(pl.multiple_of(cc * adj_rows + at, 16), size), :]

    adj_load.wait()
    adj_at = pl.ds(pl.multiple_of(code_rows + c * own, 16), own)
    for p in range(points):
        cut = slice(p * objs, (p + 1) * objs)
        high = adj_own[p].astype(BF16)
        adjg[z, adj_at, cut] = high
        adj_low[:, cut] = (adj_own[p] - high.astype(F32)).astype(BF16)
    code_at = pl.ds(pl.multiple_of(c * (2 * own + code_rows), 16), code_rows)
    for j in range(slots // 8):
        cut = slice(8 * j, 8 * j + 8)
        codes = jnp.concatenate([owner[cut], inside[cut]], axis=0)
        adjg[z, code_at, j * LANES : (j + 1) * LANES] = codes.astype(BF16)

    for load in loads:
        load.wait()
    pl.semaphore_wait(barrier, len(greeted))

    piece = own // TURNS
    waiting_ghost = []

    def ghost_at(zz, cc):
        return pl.ds(pl.multiple_of((zz * 2 + cc) * GHOST, GHOST), GHOST)

    def pass_ghost(zz):
        src = block(zz, c, 0, GHOST)
        for to in (0, 1):
            for cc in (c, other):
                device = {"grp": sides[to], "dev": z * 2 + cc}
                at = copies.start(src, ghost.at[to, ghost_at(zz, c), :], device)
                waiting_ghost.append((at, to, zz, cc, device))

    def forward_row(flow, zz, part):
        ref = block(zz, c, part * piece, piece)
        return copies.start(ref, ref, ring[flow])

    def share_row(zz):
        ref = block(zz, c)
        return copies.start(ref, ref, partner), zz

    def part_of(flow, turn):
        return (TURNS - turn) % TURNS if flow else turn

    def goes_far(flow, part):
        return (part >= TURNS // 2) == (flow == 1)

    pieces = {}
    for turn in range(TURNS):
        for flow in (0, 1):
            if far > 1 or goes_far(flow, part_of(flow, turn)):
                pieces[flow, turn] = forward_row(flow, z, part_of(flow, turn))
    shared = [share_row(z)]
    far_ghost = []
    for to in (0, 1):
        device = {"grp": sides[to], "dev": chip(far) * 2 + c}
        far_ghost.append((copies.start(block(z, c, 0, GHOST), ghost.at[to, ghost_at(z, c), :], device), to, device))
    pass_ghost(z)
    def add_tile(load, base, depth, first=False):
        base = jnp.asarray(base, jnp.int32).astype(F32)

        def body(step, carry):
            at = pl.ds(pl.multiple_of(step * PER_STEP, PER_STEP), PER_STEP)
            relative = idxb[at, :] - base
            parts = []
            for lane in range(0, depth, LANES):
                wide = min(LANES, depth - lane)
                lanes = (lax.broadcasted_iota(jnp.int32, (PER_STEP, wide), 1) + lane).astype(F32)
                parts.append(jnp.where(relative[:, :wide] == lanes, 1.0, 0.0).astype(BF16))
            hot = parts[0] if len(parts) == 1 else jnp.concatenate(parts, axis=1)
            total = jnp.dot(hot, load(), preferred_element_type=F32).astype(BF16)
            near[at, :] = total if first else near[at, :] + total
            return carry

        lax.fori_loop(0, near.shape[0] // PER_STEP, body, 0)

    def chip_tile(zz, first=False):
        add_tile(lambda: pool[zz], zz * (2 * own), 2 * own, first)

    def take_shared(found):
        for at, zz in found:
            copies.arrived(at, block(zz, other), partner)

    def take(hop, turn):
        for flow, zz in ((0, chip(-hop)), (1, chip(hop))):
            if (flow, turn) not in pieces:
                continue
            part = part_of(flow, turn)
            copies.arrived(pieces[flow, turn], block(zz, c, part * piece, piece), ring[flow])
            if hop < far - 1 or (hop == far - 1 and goes_far(flow, part)):
                later[flow, turn] = forward_row(flow, zz, part)
            if hop < far and part == 0:
                pass_ghost(zz)

    adj_first = adj_rows // 2 // 16 * 16
    adj_cut = ((0, adj_first), (adj_first, adj_rows - adj_first))
    adj_sent, adj_shared = {}, {hop: [] for hop in range(far + 1)}

    def adj_send(flow, zz, hop, turn):
        ref = adj_block(zz, c, *adj_cut[turn ^ flow])
        adj_sent[flow, hop, turn] = copies.start(ref, ref, ring[flow])

    def adj_start(turn):
        if far > 1 or turn == 0:
            for flow in (0, 1):
                adj_send(flow, z, 1, turn)

    def adj_share(hop, zz):
        ref = adj_block(zz, c)
        adj_shared[hop].append((copies.start(ref, ref, partner), zz))

    def adj_take(hop, turn):
        if hop > far:
            return
        for flow, zz in ((0, chip(-hop)), (1, chip(hop))):
            if (flow, hop, turn) in adj_sent:
                copies.arrived(adj_sent[flow, hop, turn], adj_block(zz, c, *adj_cut[turn ^ flow]), ring[flow])
                if hop < far - 1 or (hop == far - 1 and turn == 0):
                    adj_send(flow, zz, hop + 1, turn)
            if hop < far and turn == 1:
                adj_share(hop, zz)
        if hop == far and turn == 0:
            adj_share(hop, chip(hop))

    if far <= 2:
        adj_start(0)
    waiting_tiles = [z]
    for hop in range(1, far):
        later = {}
        for turn in range(TURNS // 2):
            take(hop, turn)
        take_shared(shared)
        chip_tile(waiting_tiles.pop(0), first=hop == 1)
        for turn in range(TURNS // 2, TURNS):
            take(hop, turn)
        pieces = later
        now = [chip(-hop), chip(hop)]
        shared = [share_row(zz) for zz in now]
        if hop == far - 2:
            adj_start(0)
        if hop == far - 1:
            adj_take(1, 0)
            adj_start(1)
        for zz in waiting_tiles:
            chip_tile(zz)
        waiting_tiles = now
    relayed = []
    for at, to, device in far_ghost:
        ref = ghost.at[to, ghost_at(chip(far), c), :]
        copies.arrived(at, ref, device)
        relayed.append((copies.start(ref, ref, partner), to))
    adj_share(0, z)
    take_shared(shared)
    chip_tile(waiting_tiles[0], first=far == 1)
    for zz in waiting_tiles[1:]:
        chip_tile(zz)
    for turn in range(TURNS):
        take(far, turn)
    shared = [share_row(chip(far))]
    if far == 1:
        adj_take(1, 0)
    adj_take(1, 1)
    adj_take(2, 0)
    for at, to, zz, cc, device in waiting_ghost:
        copies.arrived(at, ghost.at[to, ghost_at(zz, cc), :], device)
    for at, to in relayed:
        copies.arrived(at, ghost.at[to, ghost_at(chip(far), other), :], partner)
    side_rows = n_dev * GHOST
    add_tile((lambda: ghost[0]), n_dev * own, side_rows)
    take_shared(shared)
    chip_tile(chip(far))
    adj_take(2, 1)
    add_tile((lambda: ghost[1]), n_dev * own + side_rows, side_rows)
    adj_take(3, 0)

    lane = lax.broadcasted_iota(jnp.int32, (slots, LANES), 1)
    sub = lax.broadcasted_iota(jnp.int32, (slots, LANES), 0)
    ridge = jnp.zeros((slots, LANES), F32)
    for member in range(MEMBERS):
        ridge = jnp.where(lane - member * slots == sub, ridge_share * width, ridge)
    lane8 = lax.broadcasted_iota(jnp.int32, (8, LANES), 1)
    row8 = lax.broadcasted_iota(jnp.int32, (8, LANES), 0)
    own_mask = (lane8 >= row8 * slots) & (lane8 < row8 * slots + slots)

    def make_gram(m, carry):
        tile = near[pl.ds(pl.multiple_of(m * LANES, LANES), LANES), :]
        for p in range(points):
            part = tile[:, p * width : (p + 1) * width]
            full = lax.dot_general(part, part, (((1,), (1,)), ((), ())), preferred_element_type=F32)
            packed = full[:slots]
            for member in range(1, MEMBERS):
                packed = jnp.where(lane >= member * slots, full[member * slots : (member + 1) * slots], packed)
            at = (p * 32 + m) * 32
            gram[pl.ds(pl.multiple_of(at, 32), slots), :] = packed + ridge
            target = jnp.sum(jnp.where(own_mask, full[MEMBERS * slots :], 0.0), axis=0, keepdims=True)
            gram[pl.ds(pl.multiple_of(at + slots, 8), 8), :] = jnp.broadcast_to(target, (8, LANES))
        return carry

    lax.fori_loop(0, n_groups // 2, make_gram, 0, unroll=UNROLL_GRAM)
    lax.fori_loop(n_groups // 2, n_groups, make_gram, 0, unroll=UNROLL_GRAM)
    adj_take(3, 1)

    for i in range(slots + 1):
        turned = jnp.transpose(gram[pl.ds(i, 64, stride=32), :])
        mat[i, :, :, 0:64] = turned[: MEMBERS * slots].reshape(MEMBERS, slots, 64)

    for j0 in range(0, slots, 8):
        span = slots - j0
        at_slot = lax.broadcasted_iota(jnp.int32, (MEMBERS, span, LANES), 1) + j0

        def eliminate(step, carry):
            col = step + j0
            pivot_row = mat[col, :, j0:slots, :]
            inverse = 1.0 / mat[col, :, pl.ds(col, 1), :]
            beyond = at_slot > col
            factors = jnp.where(beyond, pivot_row * inverse, 0.0)
            for i in range(j0, slots):
                block_at = i // 8 * 8
                mat[i, :, block_at:slots, :] = (
                    mat[i, :, block_at:slots, :] - factors[:, i - j0 : i - j0 + 1, :] * pivot_row[:, block_at - j0 :, :]
                )
            rhs = mat[slots, :, pl.ds(col, 1), :]
            mat[slots, :, j0:slots, :] = mat[slots, :, j0:slots, :] - rhs * factors
            return carry

        lax.fori_loop(0, 8, eliminate, 0, unroll=True)
    at_slot = lax.broadcasted_iota(jnp.int32, (MEMBERS, slots, LANES), 1)
    solved = jnp.zeros((MEMBERS, slots, LANES), F32)
    for col in range(slots - 1, -1, -1):
        line = mat[col]
        inverse = 1.0 / line[:, col : col + 1, :]
        scaled = jnp.where(at_slot > col, line * inverse, 0.0)
        known = jnp.sum(scaled * solved, axis=1, keepdims=True)
        value = mat[slots, :, col : col + 1, :] * inverse - known
        solved = jnp.where(at_slot == col, value, solved)

    coef_rows = points * slots

    def coef_block(zz, cc):
        return coefg.at[zz, pl.ds(pl.multiple_of(cc * coef_rows, 8), coef_rows), :]

    for p in range(points):
        coeff = jnp.zeros((slots, LANES), F32)
        for member in range(MEMBERS):
            first = member * n_groups
            rolled = pltpu.roll(solved[member], (first - 32 * p) % LANES, 1)
            coeff = jnp.where((lane >= first) & (lane < first + n_groups), rolled, coeff)
        coefg[z, pl.ds(pl.multiple_of(c * coef_rows + p * slots, 8), slots), :] = coeff

    coef_sent = {}
    for hop in sorted(range(1, far + 1), key=lambda hop: hop):
        for step in (hop, -hop) if hop < far else (hop,):
            ref = coef_block(z, c)
            coef_sent[step] = copies.start(ref, ref, peer(step))

    def coef_share(zz):
        ref = coef_block(zz, c)
        return copies.start(ref, ref, partner), zz

    shared = [coef_share(z)]
    me_f = me_d.astype(F32)
    entry = lax.broadcasted_iota(jnp.int32, (ext, LANES), 0).astype(F32)

    def make_table(zz, cc):
        code_at = pl.multiple_of(cc * (2 * own + code_rows), 16)
        picked = []
        for j in range(slots // 8):
            codes = adjg[zz, pl.ds(code_at, code_rows), j * LANES : (j + 1) * LANES].astype(F32)
            picked.append(jnp.where(codes[:8] == me_f, codes[8:], -1.0))
        weights = coefg[zz, pl.ds(pl.multiple_of(cc * coef_rows, 8), coef_rows), :]
        tables = [jnp.zeros((ext, LANES), F32) for _ in range(points)]
        for k in range(slots):
            match = picked[k // 8][k % 8 : k % 8 + 1] == entry
            for p in range(points):
                row = p * slots + k
                tables[p] = tables[p] + jnp.where(match, weights[row : row + 1], 0.0)
        at = pl.ds(pl.multiple_of((zz * 2 + cc) * LANES, LANES), LANES)
        for p in range(points):
            high = tables[p].astype(BF16)
            tall[p, 0:ext, at] = high
            tall[p, ext : 2 * ext, at] = (tables[p] - high.astype(F32)).astype(BF16)

    def table_loop(hop, cc, count):
        def body(i, carry):
            make_table(jnp.where(i == 0, chip(-hop), chip(hop)), cc)
            return carry

        lax.fori_loop(0, count, body, 0)

    def take_coef(found):
        for at, zz in found:
            copies.arrived(at, coef_block(zz, other), partner)

    make_table(z, c)
    take_coef(shared)

    def take_adj(hop):
        for at, zz in adj_shared[hop]:
            copies.arrived(at, adj_block(zz, other), partner)

    take_adj(0)
    make_table(z, other)
    own_lanes = pl.ds(pl.multiple_of(me_d * LANES, LANES), LANES)

    def multiply(zz, first=False):
        lanes = pl.ds(pl.multiple_of(zz * 2 * LANES, 2 * LANES), 2 * LANES)
        for p in range(points):
            cut = slice(p * objs, (p + 1) * objs)
            product = jnp.dot(tall[p, :, lanes], adjg[zz, code_rows : code_rows + 2 * own, cut],
                              preferred_element_type=F32)
            product = product[:ext] + product[ext:]
            if first:
                acc[p] = product + jnp.dot(tall[p, :ext, own_lanes], adj_low[:, cut], preferred_element_type=F32)
            else:
                acc[p] = acc[p] + product

    multiply(z, first=True)

    def second_half(hop, found):
        take_coef(found)
        take_adj(hop)
        table_loop(hop, other, len(found))
        for _, zz in found:
            multiply(zz)

    before = []
    for hop in range(1, far + 1):
        shared = []
        for step in (-hop, hop) if hop < far else (hop,):
            copies.arrived(coef_sent[-step if hop < far else step], coef_block(chip(step), c), peer(step))
            shared.append(coef_share(chip(step)))
        if hop == 4:
            adj_take(4, 0)
        table_loop(hop, c, len(shared))
        if before:
            second_half(hop - 1, before)
        before = shared
    second_half(far, before)

    low_rows, high_rows = acc.at[:, own : own + GHOST, :], acc.at[:, own + GHOST : ext, :]
    from_above = copies.start(low_rows, back.at[0], {"grp": below})
    from_below = copies.start(high_rows, back.at[1], {"grp": above})
    out_ref[...] = adj_own[...] - acc[:, :own, :]
    copies.arrived(from_above, back.at[0], {"grp": below})
    copies.arrived(from_below, back.at[1], {"grp": above})
    out_ref[:, :GHOST, :] = out_ref[:, :GHOST, :] - (back[0] + back[1])
    copies.finish()


def local(rows, adj_rhs, pattern, lengths):
    points, own, width = rows.shape
    slots = pattern.shape[1]
    objs = adj_rhs.shape[2]
    n_grp, n_dev = lax.axis_size("grp"), lax.axis_size("dev")
    n_z = n_dev // 2
    n_groups = -(-own // MEMBERS)
    ext = own + 2 * GHOST
    n_copies = 120
    vmem = pl.BlockSpec(memory_space=pltpu.VMEM)
    anywhere = pl.BlockSpec(memory_space=pl.ANY)
    return pl.pallas_call(
        functools.partial(kernel, (n_grp, n_dev, points, own, width, slots, objs)),
        out_shape=jax.ShapeDtypeStruct(adj_rhs.shape, F32),
        in_specs=[anywhere, anywhere, vmem, vmem],
        out_specs=vmem,
        scratch_shapes=[
            pltpu.VMEM((n_z, 2 * own, points * width), BF16),
            pltpu.VMEM((2, n_dev * GHOST, points * width), BF16),
            pltpu.VMEM((n_groups * LANES, LANES), F32),
            pltpu.VMEM((n_groups * LANES, points * width), BF16),
            pltpu.VMEM((n_z, 2 * own + 32, points * objs), BF16),
            pltpu.VMEM((own, points * objs), BF16),
            pltpu.VMEM((n_z, 2 * points * slots, LANES), F32),
            pltpu.VMEM((64 * 32, LANES), F32),
            pltpu.VMEM((slots + 1, MEMBERS, slots, LANES), F32),
            pltpu.VMEM((points, 2 * ext, n_dev * LANES), BF16),
            pltpu.VMEM((points, own, objs), F32),
            pltpu.VMEM((points, ext, objs), F32),
            pltpu.VMEM((2, points, GHOST, objs), F32),
            pltpu.SemaphoreType.DMA((n_copies,)),
            pltpu.SemaphoreType.DMA((n_copies,)),
            pltpu.SemaphoreType.DMA((points + 1,)),
        ],
        compiler_params=pltpu.CompilerParams(
            collective_id=0, has_side_effects=True, vmem_limit_bytes=48 * 1024 * 1024
        ),
    )(rows, adj_rhs, pattern, lengths.reshape(1, own))


def solution(mesh):
    placed = (
        P(None, ("grp", "dev"), None),
        P(None, ("grp", "dev"), None),
        P(("grp", "dev"), None),
        P(("grp", "dev")),
    )
    return jax.shard_map(
        local, mesh=mesh, in_specs=placed, out_specs=P(None, ("grp", "dev"), None), check_vma=False
    )
```
